256 devices in a mesh: src: 64 (over x, z, core), tgt: 4 (over y).
Axes of the slice: x: 4, y: 4, z: 8, core: 2. Of those that a mesh axis runs over, the one named last changes fastest.
Arguments:
- source: bfloat16 [65536, 300], P('src'), may hold values from -8 to 8
- target: bfloat16 [8192, 300], P(('tgt', 'src')), may hold values from -8 to 8
- rotation: bfloat16 [300, 300], replicated, may hold values from -0.5 to 1.5
Outputs:
- src_potential: float32 [65536], P('src')
- tgt_potential: float32 [8192], P('tgt')
- matched: float32 [65536, 300], P('src', 'tgt')
- rotation_grad: float32 [300, 300], replicated
The draws below stay inside these ranges and needn't reach their ends.
All inputs are finite; a program needn't handle non-finite values.
Results may differ from the reference program's by a relative error of at most 0.0003.
The reference program's roundings to bfloat16 on the way (of `rotated` and `weights`) count: a program that leaves them out, or rounds other values in their place, can miss the bound.
Values may be sent and summed in bfloat16 or wider, within the bound.
A program may use at most 64 MiB of HBM per device.

```python
import math
import jax
import jax.numpy as jnp
from jax import lax

D = 300
SWEEPS = 2
NS = 65536
NT = 8192


def strong_rows(key):
    sub = jax.random.fold_in(key, 41)
    signs = jax.random.bernoulli(sub, 0.5, (8, D))
    return jnp.where(signs, 8.0, -8.0).astype(jnp.float32)


def draw_target(key, part):
    base = key
    key = jax.random.fold_in(key, 5)
    first = jax.random.fold_in(key, 0)
    third = jax.random.fold_in(key, 2)
    fourth = jax.random.fold_in(key, 3)
    values = jnp.clip(jax.random.normal(first, (NT, D)), -6.0, 6.0)
    picks = jax.random.randint(third, (8,), 0, NT // 2) * 2
    strong = strong_rows(base)
    near = jnp.clip(strong + 0.5 * jax.random.normal(fourth, (8, D)), -8.0, 8.0)
    values = values.at[picks].set(strong).at[picks + 1].set(near)
    return values.astype(jnp.bfloat16)


def draw_source(key, part):
    base = key
    key = jax.random.fold_in(key, 7)
    first = jax.random.fold_in(key, 0)
    third = jax.random.fold_in(key, 2)
    values = jnp.clip(jax.random.normal(first, (NS, D)), -6.0, 6.0)
    places = jax.random.randint(third, (8,), 0, NS)
    factors = jnp.array([1.0, 0.9, 0.8, 0.7, 0.6, 1.0, 0.8, 0.65], jnp.float32)
    values = values.at[places].set(factors[:, None] * strong_rows(base))
    return values.astype(jnp.bfloat16)


def draw_rotation(key, part):
    key = jax.random.fold_in(key, 9)
    noise = jnp.clip(jax.random.normal(key, (D, D)), -4.0, 4.0) * (0.3 / math.sqrt(D))
    return (jnp.eye(D, dtype=jnp.float32) + noise).astype(jnp.bfloat16)


def setup_inputs(seed: int = 0) -> dict:
    splits = jax.random.split(jax.random.key(seed), 4)
    source = draw_source(jax.random.fold_in(splits[3], 71), 0)
    target = draw_target(jax.random.fold_in(splits[3], 71), 0)
    rotation = draw_rotation(jax.random.fold_in(splits[3], 71), 0)
    return dict(source=source, target=target, rotation=rotation)


epsilon = 2.0

def reference(source, target, rotation):
    rotated = jnp.dot(target, rotation.T, preferred_element_type=jnp.float32).astype(jnp.bfloat16)
    block = math.gcd(NS, 1024)
    count = NS // block
    src_blocks = source.reshape(count, block, D)
    inv_root = 1.0 / math.sqrt(D)

    def cost_rows(rows):
        return -jnp.dot(rows, rotated.T, preferred_element_type=jnp.float32) * inv_root
    cost = lax.map(cost_rows, src_blocks)
    src_potential = jnp.zeros((NS,), jnp.float32)
    tgt_potential = jnp.zeros((NT,), jnp.float32)
    for sweep in range(SWEEPS):
        pot_blocks = src_potential.reshape(count, block)

        def col_step(carry, pieces):
            top, total = carry
            cost_block, pot = pieces
            scaled = (pot[:, None] - cost_block) / epsilon
            new_top = jnp.maximum(top, lax.optimization_barrier(jnp.max(scaled, axis=0)))
            total = total * jnp.exp(top - new_top) + lax.optimization_barrier(jnp.sum(jnp.exp(scaled - new_top[None, :]), axis=0))
            return ((new_top, total), None)
        start = (jnp.full((NT,), -jnp.inf, jnp.float32), jnp.zeros((NT,), jnp.float32))
        (top, total), unused = lax.scan(col_step, start, (cost, pot_blocks))
        tgt_potential = epsilon * math.log(NS) - epsilon * (top + jnp.log(total))

        def row_lse(cost_block):
            return jax.nn.logsumexp((tgt_potential[None, :] - cost_block) / epsilon, axis=1)
        src_potential = epsilon * math.log(NT) - epsilon * lax.map(row_lse, cost).reshape(NS)

    def plan_rows(pieces):
        cost_block, pot = pieces
        weights = jnp.exp((pot[:, None] + tgt_potential[None, :] - cost_block) / epsilon).astype(jnp.bfloat16)
        return jnp.dot(weights, target, preferred_element_type=jnp.float32) / NT
    matched = lax.map(plan_rows, (cost, src_potential.reshape(count, block))).reshape(NS, D)
    rotation_grad = epsilon * math.sqrt(D) / NS * jnp.dot(source.astype(jnp.float32).T, matched, precision=lax.Precision.HIGHEST)
    return (src_potential, tgt_potential, matched, rotation_grad)
```

```python
import functools
import math

import jax
import jax.numpy as jnp
from jax import lax
from jax.experimental import pallas as pl
from jax.experimental.pallas import tpu as pltpu
from jax.sharding import PartitionSpec as P

MESH = pl.DeviceIdType.MESH
F32 = jnp.float32
BF16 = jnp.bfloat16

XS, ZS, YS = 4, 8, 4
CHIPS = XS * ZS
D = 300
ROWS = 1024
COLS = 2048
NS, NT = 65536, 8192
EPS = 2.0
LN2 = math.log(2.0)
SLAB = 80
WIDE = YS * SLAB
CHUNK = 512
TILES = 64
NTD = (((1,), (1,)), ((), ()))
NND = (((1,), (0,)), ((), ()))


def dot(a, b, dims):
    return lax.dot_general(a, b, dims, preferred_element_type=F32)


def kernel(
    src_ref, tgt_ref, rot_ref,
    f_ref, g_ref, m_ref, grad_ref,
    G, R, GT, S, W, MT, RM, TOPB, RB,
    CV, CP, CX, CR, CF, GV,
    RV, RR, FV,
    GP, GB, GC, GS, GR, GO, GY, GZ, GF,
    gather_send, gather_recv, fwd_send, core_send,
    cp_send, cp_recv, cx_send, cx_recv, cf_send, cf_recv,
    rr_send, rr_recv, rm_send, rm_recv,
    gc_send, gc_recv, gr_send, gr_recv, gy_send, gy_recv, gz_send, gz_recv, gf_send, gf_recv,
):
    s = lax.axis_index("src")
    y = lax.axis_index("tgt")
    idx = s // 2
    c = s % 2
    x = idx // ZS
    z = idx % ZS
    mate = {"src": idx * 2 + (1 - c)}

    def chip(p):
        return {"src": p * 2 + c}

    def copy(a, b, ss, rs, to):
        return pltpu.make_async_remote_copy(
            src_ref=a, dst_ref=b, send_sem=ss, recv_sem=rs, device_id=to, device_id_type=MESH
        )

    barrier = pltpu.get_barrier_semaphore()

    @pl.loop(1, CHIPS)
    def _(d):
        pl.semaphore_signal(barrier, inc=1, device_id=chip((idx + d) % CHIPS), device_id_type=MESH)

    pl.semaphore_signal(barrier, inc=1, device_id=mate, device_id_type=MESH)
    for d in range(1, YS):
        pl.semaphore_signal(barrier, inc=1, device_id={"tgt": (y + d) % YS}, device_id_type=MESH)
    pl.semaphore_wait(barrier, CHIPS - 1 + 1 + YS - 1)

    def z_copy(d):
        return copy(
            tgt_ref, G.at[idx, c], gather_send.at[d], gather_recv.at[idx, c],
            chip(x * ZS + (z + d) % ZS),
        )

    def x_copy(p, d, k):
        return copy(
            G.at[p, c], G.at[p, c], fwd_send.at[d, k], gather_recv.at[p, c],
            chip(((x + d) % XS) * ZS + z),
        )

    def core_copy(xc, k):
        block = G.at[pl.ds(xc * ZS, ZS), c]
        return copy(block, block, core_send.at[k], gather_recv.at[xc * ZS, c], mate)

    def core_wait(xc, k):
        block = G.at[pl.ds(xc * ZS, ZS), 1 - c]
        copy(block, block, core_send.at[k], gather_recv.at[xc * ZS, 1 - c], mate).wait_recv()

    def arrived(p):
        copy(
            tgt_ref, G.at[p, c], gather_send.at[0], gather_recv.at[p, c], mate
        ).wait_recv()

    z_order = (1, 7, 2, 6, 3, 5, 4)
    x_order = (1, 3, 2)
    for d in z_order:
        z_copy(d).start()
    G[idx, c] = tgt_ref[...]
    for d in x_order:
        x_copy(idx, d, 0).start()
    for d in z_order:
        p = x * ZS + (z + d) % ZS
        arrived(p)
        for e in x_order:
            x_copy(p, e, d).start()
    core_copy(x, 0).start()

    a = lax.broadcasted_iota(jnp.int32, (WIDE, D), 0)
    b = lax.broadcasted_iota(jnp.int32, (WIDE, D), 1)
    hit = jnp.zeros((WIDE, D), jnp.bool_)
    for q in range(YS):
        hit = hit | ((a - SLAB * q == b - 75 * q) & (b >= 75 * q) & (b < 75 * q + 75))
    spread = jnp.where(hit, 1.0, 0.0).astype(BF16)

    scale = math.log2(math.e) / (EPS * math.sqrt(D))
    HALF = 256

    def chunk_work(xc):
        cols = pl.ds(pl.multiple_of(xc * CHUNK, CHUNK), CHUNK)
        words = G[pl.ds(xc * ZS, ZS)].reshape(CHUNK, D)
        GT[:, cols] = dot(spread, words, NTD).astype(BF16)
        R[...] = dot(words, rot_ref[...], NTD).astype(BF16)

        def fill(i, top):
            rows = pl.ds(pl.multiple_of(i * HALF, HALF), HALF)
            part = dot(src_ref[rows, :], R[...], NTD) * scale
            S[rows, cols] = part
            return jnp.maximum(top, jnp.max(part.reshape(HALF // 8, 8, CHUNK), axis=0))

        top = lax.fori_loop(0, ROWS // HALF, fill, jnp.full((8, CHUNK), -jnp.inf, F32))
        top = jnp.max(top, axis=0, keepdims=True)

        def add(i, total):
            rows = pl.ds(pl.multiple_of(i * 64, 64), 64)
            e = jnp.exp2(S[rows, cols] - top)
            return total + jnp.sum(e.reshape(8, 8, CHUNK), axis=0)

        total = lax.fori_loop(0, ROWS // 64, add, jnp.zeros((8, CHUNK), F32))
        lse = top + jnp.log2(jnp.sum(total, axis=0, keepdims=True))
        for k in range(CHUNK // 128):
            CV[0, pl.ds(xc * 4 + k, 1), 0] = lse[:, k * 128 : (k + 1) * 128]

    for k, d in enumerate((0,) + x_order):
        xc = (x + d) % XS
        if d:
            for e in range(ZS):
                arrived(xc * ZS + e)
            core_copy(xc, k).start()
        core_wait(xc, k)
        chunk_work(xc)

    def lse2(u, v):
        m = jnp.maximum(u, v)
        return m + jnp.log2(jnp.exp2(u - m) + jnp.exp2(v - m))

    def cp_copy(n):
        return copy(CV.at[n, pl.ds((1 - c) * 8, 8)], CP.at[n], cp_send.at[n], cp_recv.at[n], mate)

    def cx_copy(n, d):
        p = (idx + d) % CHIPS
        return copy(CX.at[n], CR.at[n, idx], cx_send.at[n, d], cx_recv.at[n, idx], chip(p))

    def cx_wait(n, d):
        p = (idx + d) % CHIPS
        copy(CX.at[n], CR.at[n, p], cx_send.at[n, d], cx_recv.at[n, p], chip(p)).wait_recv()

    def cf_copy(n):
        half = CF.at[n, pl.ds(c * 8, 8)]
        return copy(half, half, cf_send.at[n], cf_recv.at[n], mate)

    def column_exchange(n, log):
        cp_copy(n).start()
        cp_copy(n).wait_recv()
        mine = CV[n, pl.ds(c * 8, 8)]
        CX[n] = lse2(mine, CP[n]) if log else mine + CP[n]

        @pl.loop(1, CHIPS)
        def _(d):
            cx_copy(n, d).start()

        CR[n, pl.ds(idx, 1)] = CX[n][None]

        @pl.loop(1, CHIPS)
        def _(d):
            cx_wait(n, d)

        got = CR[n]
        if log:
            m = jnp.max(got, axis=0)
            half = m + jnp.log2(jnp.sum(jnp.exp2(got - m[None]), axis=0))
        else:
            half = jnp.sum(got, axis=0)
        CF[n, pl.ds(c * 8, 8)] = half
        cf_copy(n).start()
        cf_copy(n).wait_recv()

    column_exchange(0, True)
    for k in range(COLS // 128):
        GV[:, k * 128 : (k + 1) * 128] = math.log2(NS) - CF[0, k]

    eye = lax.broadcasted_iota(jnp.int32, (128, 128), 0) == lax.broadcasted_iota(
        jnp.int32, (128, 128), 1
    )

    def to_row(col):
        return jnp.sum(jnp.where(eye, col, 0.0), axis=0, keepdims=True)

    def to_col(row):
        return jnp.sum(jnp.where(eye, row, 0.0), axis=1, keepdims=True)

    def lanes(v):
        out = v[:, 0:128]
        for k in range(1, COLS // 128):
            out = out + v[:, k * 128 : (k + 1) * 128]
        return out

    STEP = 16

    def row_one(i, _):
        rows = pl.ds(pl.multiple_of(i * STEP, STEP), STEP)
        v = S[rows, :] + GV[...]
        top = jnp.max(v, axis=1, keepdims=True)
        e = jnp.exp2(v - top)
        S[rows, :] = e
        RB[rows, :] = lanes(e)
        TOPB[rows, :] = jnp.broadcast_to(top, (STEP, 128))
        return 0

    lax.fori_loop(0, ROWS // STEP, row_one, 0, unroll=2)

    def rr_copy(n, d):
        return copy(
            RV.at[n], RR.at[n, y], rr_send.at[n, d], rr_recv.at[n, y], {"tgt": (y + d) % YS}
        )

    def rr_wait(n, d):
        p = (y + d) % YS
        copy(RV.at[n], RR.at[n, p], rr_send.at[n, d], rr_recv.at[n, p], {"tgt": p}).wait_recv()

    def row_exchange(n):
        for d in range(1, YS):
            rr_copy(n, d).start()
        RR[n, pl.ds(y, 1)] = RV[n][None]
        for d in range(1, YS):
            rr_wait(n, d)
        return RR[n]

    for k in range(ROWS // 128):
        rows = pl.ds(k * 128, 128)
        total = jnp.sum(RB[rows, :], axis=1, keepdims=True)
        RV[0, k : k + 1] = to_row(TOPB[rows, :] + jnp.log2(total))
    got = row_exchange(0)
    m = jnp.max(got, axis=0)
    lse = m + jnp.log2(jnp.sum(jnp.exp2(got - m[None]), axis=0))
    FV[...] = math.log2(NT) - lse
    for k in range(ROWS // 128):
        rows = pl.ds(k * 128, 128)
        RB[rows, :] = jnp.exp2(TOPB[rows, :] + to_col(FV[k : k + 1, :]))

    def col_two(i, total):
        rows = pl.ds(pl.multiple_of(i * STEP, STEP), STEP)
        r = RB[rows, :]
        e = S[rows, :] * jnp.concatenate([r] * (COLS // 128), axis=1)
        S[rows, :] = e
        return total + e[0:8] + e[8:16]

    total = lax.fori_loop(0, ROWS // STEP, col_two, jnp.zeros((8, COLS), F32))
    total = jnp.sum(total, axis=0, keepdims=True)
    for k in range(COLS // 128):
        CV[1, k] = total[:, k * 128 : (k + 1) * 128]
    column_exchange(1, False)
    for k in range(COLS // 128):
        u = CF[1, k]
        g_ref[k] = (EPS * LN2) * (GV[:, k * 128 : (k + 1) * 128] + (math.log2(NS) - jnp.log2(u)))
        GV[:, k * 128 : (k + 1) * 128] = NS / u

    def row_two(i, _):
        rows = pl.ds(pl.multiple_of(i * STEP, STEP), STEP)
        e = S[rows, :] * GV[...]
        S[rows, :] = e
        RB[rows, :] = lanes(e)
        return 0

    lax.fori_loop(0, ROWS // STEP, row_two, 0)
    for k in range(ROWS // 128):
        rows = pl.ds(k * 128, 128)
        RV[1, k : k + 1] = to_row(jnp.sum(RB[rows, :], axis=1, keepdims=True))
    got = row_exchange(1)
    rho = (got[0] + got[1]) + (got[2] + got[3])
    f_ref[...] = (EPS * LN2) * (FV[...] + (math.log2(NT) - jnp.log2(rho)))
    FV[...] = NT / rho
    for k in range(ROWS // 128):
        rows = pl.ds(k * 128, 128)
        RB[rows, :] = jnp.broadcast_to(to_col(FV[k : k + 1, :]), (128, 128))

    MC = 256

    def rm_copy(k, d):
        p = (y + d) % YS
        cols = pl.ds(k * MC, MC)
        return copy(
            MT.at[pl.ds(pl.multiple_of(p * SLAB, 8), SLAB), cols], RM.at[d - 1, :, cols],
            rm_send.at[k, d], rm_recv.at[k, d], {"tgt": p},
        )

    for k in range(ROWS // MC):

        def weigh(i, _, k=k):
            rows = pl.ds(pl.multiple_of(k * MC + i * STEP, STEP), STEP)
            r = RB[rows, :]
            e = S[rows, :] * jnp.concatenate([r] * (COLS // 128), axis=1)
            W[pl.ds(pl.multiple_of(i * STEP, STEP), STEP), :] = e.astype(BF16)
            return 0

        lax.fori_loop(0, MC // STEP, weigh, 0)
        MT[:, k * MC : (k + 1) * MC] = dot(GT[...], W[...], NTD) * (1.0 / NT)
        for d in (2, 1, 3):
            rm_copy(k, d).start()

    grad = jnp.zeros((WIDE, D), F32)
    rest = MT[...]
    for part in range(3):
        piece = rest.astype(BF16)
        grad = grad + dot(piece, src_ref[...], NND)
        rest = rest - piece.astype(F32)
    GP[...] = jnp.zeros_like(GP)
    GP[:, 0:D] = grad * (EPS * math.sqrt(D) / NS)
    GB[...] = jnp.zeros_like(GB)
    for h in range(2):
        for t in range(3):
            GB[h, t * 20 : (t + 1) * 20] = GP[
                h * 160 : (h + 1) * 160, t * 128 : (t + 1) * 128
            ].reshape(20, 8, 128)

    gc = copy(GB.at[1 - c], GC, gc_send, gc_recv, mate)
    gc.start()
    gc.wait_recv()
    GS[...] = (GB[c] + GC[...]).reshape(CHIPS, 2, 8, 128)

    def gr_copy(d):
        p = (idx + d) % CHIPS
        return copy(GS.at[p], GR.at[idx], gr_send.at[d], gr_recv.at[idx], chip(p))

    def gr_wait(d):
        p = (idx + d) % CHIPS
        copy(GS.at[p], GR.at[p], gr_send.at[d], gr_recv.at[p], chip(p)).wait_recv()

    @pl.loop(1, CHIPS)
    def _(d):
        gr_copy(d).start()

    GR[pl.ds(idx, 1)] = GS[pl.ds(idx, 1)]

    @pl.loop(1, CHIPS)
    def _(d):
        gr_wait(d)

    GO[...] = jnp.sum(GR[...], axis=0)

    def gy_copy(d):
        return copy(GO, GY.at[y], gy_send.at[d], gy_recv.at[y], {"tgt": (y + d) % YS})

    def gy_wait(d):
        p = (y + d) % YS
        copy(GO, GY.at[p], gy_send.at[d], gy_recv.at[p], {"tgt": p}).wait_recv()

    for d in range(1, YS):
        gy_copy(d).start()
    GY[pl.ds(y, 1)] = GO[...][None]
    for d in range(1, YS):
        gy_wait(d)
    GZ[...] = (GY[0] + GY[1]) + (GY[2] + GY[3])

    def gz_copy(d):
        p = (idx + d) % CHIPS
        return copy(GZ, GF.at[c, idx], gz_send.at[d], gz_recv.at[idx], chip(p))

    def gz_wait(d):
        p = (idx + d) % CHIPS
        copy(GZ, GF.at[c, p], gz_send.at[d], gz_recv.at[p], chip(p)).wait_recv()

    @pl.loop(1, CHIPS)
    def _(d):
        gz_copy(d).start()

    GF[c, pl.ds(idx, 1)] = GZ[...][None]

    for k in range(ROWS // MC):
        for d in range(1, YS):
            rm_copy(k, d).wait_recv()
    own = MT[pl.ds(pl.multiple_of(y * SLAB, 8), SLAB), :]
    m_ref[...] = (own + RM[0]) + (RM[1] + RM[2])

    @pl.loop(1, CHIPS)
    def _(d):
        gz_wait(d)

    gf = copy(GF.at[c], GF.at[c], gf_send, gf_recv, mate)
    gf.start()
    gf.wait_recv()
    for h in range(2):
        flat = GF[h].reshape(TILES, 8, 128)
        for t in range(3):
            wide = min(128, D - t * 128)
            grad_ref[h * 160 : (h + 1) * 160, t * 128 : t * 128 + wide] = flat[
                t * 20 : (t + 1) * 20
            ].reshape(160, 128)[:, 0:wide]

    for d in z_order:
        z_copy(d).wait_send()
    for d in x_order:
        for k in range(ZS):
            x_copy(x * ZS + (z + k) % ZS, d, k).wait_send()
    for k, d in enumerate((0,) + x_order):
        core_copy((x + d) % XS, k).wait_send()
    for n in range(2):
        cp_copy(n).wait_send()
        cf_copy(n).wait_send()
        for d in range(1, YS):
            rr_copy(n, d).wait_send()
    for d in range(1, YS):
        gy_copy(d).wait_send()
        for k in range(ROWS // MC):
            rm_copy(k, d).wait_send()
    gc.wait_send()
    gf.wait_send()

    @pl.loop(1, CHIPS)
    def _(d):
        cx_copy(0, d).wait_send()
        cx_copy(1, d).wait_send()
        gr_copy(d).wait_send()
        gz_copy(d).wait_send()


def shards(source, target, rotation):
    vmem = pl.BlockSpec(memory_space=pltpu.VMEM)
    dma = pltpu.SemaphoreType.DMA
    scratch = [
        pltpu.VMEM((CHIPS, 2, 32, D), BF16),
        pltpu.VMEM((CHUNK, D), BF16),
        pltpu.VMEM((WIDE, COLS), BF16),
        pltpu.VMEM((ROWS, COLS), F32),
        pltpu.VMEM((256, COLS), BF16),
        pltpu.VMEM((WIDE, ROWS), F32),
        pltpu.VMEM((YS - 1, SLAB, ROWS), F32),
        pltpu.VMEM((ROWS, 128), F32),
        pltpu.VMEM((ROWS, 128), F32),
        pltpu.VMEM((2, 16, 1, 128), F32),
        pltpu.VMEM((2, 8, 1, 128), F32),
        pltpu.VMEM((2, 8, 1, 128), F32),
        pltpu.VMEM((2, CHIPS, 8, 1, 128), F32),
        pltpu.VMEM((2, 16, 1, 128), F32),
        pltpu.VMEM((1, COLS), F32),
        pltpu.VMEM((2, 8, 128), F32),
        pltpu.VMEM((2, YS, 8, 128), F32),
        pltpu.VMEM((8, 128), F32),
        pltpu.VMEM((WIDE, 384), F32),
        pltpu.VMEM((2, TILES, 8, 128), F32),
        pltpu.VMEM((TILES, 8, 128), F32),
        pltpu.VMEM((CHIPS, 2, 8, 128), F32),
        pltpu.VMEM((CHIPS, 2, 8, 128), F32),
        pltpu.VMEM((2, 8, 128), F32),
        pltpu.VMEM((YS, 2, 8, 128), F32),
        pltpu.VMEM((2, 8, 128), F32),
        pltpu.VMEM((2, CHIPS, 2, 8, 128), F32),
        dma((ZS,)), dma((CHIPS, 2)), dma((XS, ZS)), dma((XS,)),
        dma((2,)), dma((2,)), dma((2, CHIPS)), dma((2, CHIPS)), dma((2,)), dma((2,)),
        dma((2, YS)), dma((2, YS)), dma((4, YS)), dma((4, YS)),
        dma, dma, dma((CHIPS,)), dma((CHIPS,)), dma((YS,)), dma((YS,)),
        dma((CHIPS,)), dma((CHIPS,)), dma, dma,
    ]
    f, g, m, grad = pl.pallas_call(
        kernel,
        out_shape=(
            jax.ShapeDtypeStruct((8, 128), F32),
            jax.ShapeDtypeStruct((16, 1, 128), F32),
            jax.ShapeDtypeStruct((SLAB, ROWS), F32),
            jax.ShapeDtypeStruct((WIDE, D), F32),
        ),
        in_specs=[vmem] * 3,
        out_specs=(vmem,) * 4,
        scratch_shapes=scratch,
        compiler_params=pltpu.CompilerParams(
            collective_id=0, has_side_effects=True, vmem_limit_bytes=48 << 20
        ),
        name="sinkhorn_step",
    )(source, target, rotation)
    rotation_grad = grad.reshape(YS, SLAB, D)[:, :75].reshape(D, D).T
    return (f.reshape(ROWS), g.reshape(COLS), m[:75].T, rotation_grad)


def solution(mesh):
    placed = (P("src", None), P(("tgt", "src"), None), P())
    return jax.shard_map(
        shards,
        mesh=mesh,
        in_specs=placed,
        out_specs=(P("src"), P("tgt"), P("src", "tgt"), P()),
        check_vma=False,
    )
```

```python
import functools
import math

import jax
import jax.numpy as jnp
from jax import lax
from jax.experimental import pallas as pl
from jax.experimental.pallas import tpu as pltpu
from jax.sharding import PartitionSpec as P

MESH = pl.DeviceIdType.MESH
F32 = jnp.float32
BF16 = jnp.bfloat16

XS, ZS, YS = 4, 8, 4
CHIPS = XS * ZS
D = 300
ROWS = 1024
COLS = 2048
NS, NT = 65536, 8192
EPS = 2.0
LN2 = math.log(2.0)
SLAB = 80
WIDE = YS * SLAB
CHUNK = 512
RT8 = 19
TILES = 64
NTD = (((1,), (1,)), ((), ()))
NND = (((1,), (0,)), ((), ()))


def hops(d):
    return min(d // ZS, XS - d // ZS) + min(d % ZS, ZS - d % ZS)


FAR = sorted(range(1, CHIPS), key=hops, reverse=True)


def dot(a, b, dims):
    return lax.dot_general(a, b, dims, preferred_element_type=F32)


def kernel(
    src_hbm, tgt_hbm, rot_hbm,
    f_ref, g_ref, m_ref, grad_ref,
    G, ST, SRC, RQ, RT, GT, S, W, MT, RM, TOPB, RB,
    CV, CP, CX, CR, CF, GV,
    RV, RR, FV,
    GP, GB, GC, GS, GR, GO, GY, GZ, GF,
    load, gather_send, gather_recv, fwd_send, core_send, block_send,
    cp_send, cp_recv, cx_send, cx_recv, cf_send, cf_recv,
    rr_send, rr_recv, rm_send, rm_recv,
    gc_send, gc_recv, gr_send, gr_recv, gy_send, gy_recv, gz_send, gz_recv, gf_send, gf_recv,
):
    s = lax.axis_index("src")
    y = lax.axis_index("tgt")
    idx = s // 2
    c = s % 2
    x = idx // ZS
    z = idx % ZS
    mate = {"src": idx * 2 + (1 - c)}

    def chip(p):
        return {"src": p * 2 + c}

    def copy(a, b, ss, rs, to):
        return pltpu.make_async_remote_copy(
            src_ref=a, dst_ref=b, send_sem=ss, recv_sem=rs, device_id=to, device_id_type=MESH
        )

    loads = (
        pltpu.make_async_copy(tgt_hbm, G.at[idx, c], load.at[0]),
        pltpu.make_async_copy(rot_hbm, RQ, load.at[1]),
        pltpu.make_async_copy(src_hbm, ST, load.at[2]),
    )
    for one in loads:
        one.start()

    barrier = pltpu.get_barrier_semaphore()

    for d in (4, 3, 5, 2, 6, 1, 7):
        to = chip(x * ZS + (z + d) % ZS)
        pl.semaphore_signal(barrier, inc=1, device_id=to, device_id_type=MESH)
    for d in (2, 1, 3):
        to = chip(((x + d) % XS) * ZS + z)
        pl.semaphore_signal(barrier, inc=1, device_id=to, device_id_type=MESH)
        pl.semaphore_signal(barrier, inc=1, device_id={"tgt": (y + d) % YS}, device_id_type=MESH)
    pl.semaphore_signal(barrier, inc=1, device_id=mate, device_id_type=MESH)
    pl.semaphore_wait(barrier, ZS - 1 + XS - 1 + YS - 1 + 1)

    def z_copy(d):
        return copy(
            G.at[idx, c], G.at[idx, c], gather_send.at[d], gather_recv.at[idx, c],
            chip(x * ZS + (z + d) % ZS),
        )

    def x_copy(p, d, k):
        return copy(
            G.at[p, c], G.at[p, c], fwd_send.at[d, k], gather_recv.at[p, c],
            chip(((x + d) % XS) * ZS + z),
        )

    def core_copy(xc, k):
        block = G.at[pl.ds(xc * ZS, ZS), c]
        return copy(block, block, core_send.at[k], gather_recv.at[xc * ZS, c], mate)

    def block_copy(p, d):
        return copy(G.at[p, c], G.at[p, c], block_send.at[d], gather_recv.at[p, c], mate)

    def block_wait(p):
        other = G.at[p, 1 - c]
        copy(other, other, block_send.at[0], gather_recv.at[p, 1 - c], mate).wait_recv()

    def core_wait(xc, k):
        block = G.at[pl.ds(xc * ZS, ZS), 1 - c]
        copy(block, block, core_send.at[k], gather_recv.at[xc * ZS, 1 - c], mate).wait_recv()

    def arrived(p):
        copy(
            G.at[p, c], G.at[p, c], gather_send.at[0], gather_recv.at[p, c], mate
        ).wait_recv()

    z_order = (1, 7, 2, 6, 3, 5, 4)
    x_order = (1, 3, 2)
    loads[0].wait()
    for d in z_order:
        z_copy(d).start()
    for d in x_order:
        x_copy(idx, d, 0).start()
    block_copy(idx, 0).start()
    loads[1].wait()
    loads[2].wait()
    SRC[...] = ST[...].T
    a = lax.broadcasted_iota(jnp.int32, (WIDE, D), 0)
    b = lax.broadcasted_iota(jnp.int32, (WIDE, D), 1)
    hit = jnp.zeros((WIDE, D), jnp.bool_)
    for q in range(YS):
        hit = hit | ((a - SLAB * q == b - 75 * q) & (b >= 75 * q) & (b < 75 * q + 75))
    spread = jnp.where(hit, 1.0, 0.0).astype(BF16)

    for d in z_order:
        p = x * ZS + (z + d) % ZS
        arrived(p)
        for e in x_order:
            x_copy(p, e, d).start()
        block_copy(p, d).start()

    scale = math.log2(math.e) / (EPS * math.sqrt(D))
    HALF = 256

    def chunk_work(xc):
        words = G[pl.ds(xc * ZS, ZS)].reshape(CHUNK, D)
        GT[:, pl.ds(pl.multiple_of(xc * CHUNK, CHUNK), CHUNK)] = dot(spread, words, NTD).astype(BF16)
        RT[...] = dot(RQ[...], words, NTD).astype(BF16)
        for h in range(CHUNK // HALF):
            cols = pl.ds(pl.multiple_of(xc * CHUNK + h * HALF, HALF), HALF)
            part = dot(SRC[...], RT[:, h * HALF : (h + 1) * HALF], NND) * scale
            S[:, cols] = part
            top = jnp.max(part, axis=0, keepdims=True)
            total = jnp.sum(jnp.exp2(S[:, cols] - top), axis=0, keepdims=True)
            lse = top + jnp.log2(total)
            for k in range(HALF // 128):
                CV[0, pl.ds(xc * 4 + h * 2 + k, 1), 0] = lse[:, k * 128 : (k + 1) * 128]

    def forward(d):
        xc = (x + d) % XS
        for e in range(ZS):
            arrived(xc * ZS + e)
        core_copy(xc, d).start()

    def finish(d):
        xc = (x + d) % XS
        core_wait(xc, d)
        chunk_work(xc)

    for e in range(ZS):
        block_wait(x * ZS + e)
    chunk_work(x)
    forward(1)
    forward(3)
    finish(1)
    forward(2)
    finish(3)
    finish(2)

    def lse2(u, v):
        m = jnp.maximum(u, v)
        return m + jnp.log2(jnp.exp2(u - m) + jnp.exp2(v - m))

    def cp_copy(n):
        return copy(CV.at[n, pl.ds((1 - c) * 8, 8)], CP.at[n], cp_send.at[n], cp_recv.at[n], mate)

    def cx_copy(n, d):
        p = ((x + d // ZS) % XS) * ZS + (z + d % ZS) % ZS
        return copy(CX.at[n], CR.at[n, idx], cx_send.at[n, d], cx_recv.at[n, idx], chip(p))

    def cx_wait(n, d):
        p = ((x + d // ZS) % XS) * ZS + (z + d % ZS) % ZS
        copy(CX.at[n], CR.at[n, p], cx_send.at[n, d], cx_recv.at[n, p], chip(p)).wait_recv()

    def cf_copy(n):
        half = CF.at[n, pl.ds(c * 8, 8)]
        return copy(half, half, cf_send.at[n], cf_recv.at[n], mate)

    def column_exchange(n, log):
        cp_copy(n).start()
        cp_copy(n).wait_recv()
        mine = CV[n, pl.ds(c * 8, 8)]
        CX[n] = lse2(mine, CP[n]) if log else mine + CP[n]

        for d in FAR:
            cx_copy(n, d).start()

        CR[n, pl.ds(idx, 1)] = CX[n][None]

        for d in FAR[::-1]:
            cx_wait(n, d)

        got = CR[n]
        if log:
            m = jnp.max(got, axis=0)
            half = m + jnp.log2(jnp.sum(jnp.exp2(got - m[None]), axis=0))
        else:
            half = jnp.sum(got, axis=0)
        CF[n, pl.ds(c * 8, 8)] = half
        cf_copy(n).start()
        cf_copy(n).wait_recv()

    column_exchange(0, True)
    for k in range(COLS // 128):
        GV[:, k * 128 : (k + 1) * 128] = math.log2(NS) - CF[0, k]

    eye = lax.broadcasted_iota(jnp.int32, (128, 128), 0) == lax.broadcasted_iota(
        jnp.int32, (128, 128), 1
    )

    def to_row(col):
        return jnp.sum(jnp.where(eye, col, 0.0), axis=0, keepdims=True)

    def to_col(row):
        return jnp.sum(jnp.where(eye, row, 0.0), axis=1, keepdims=True)

    STEP = 16
    BLOCK = 128

    def row_one(i, _):
        rows = pl.ds(pl.multiple_of(i * BLOCK, BLOCK), BLOCK)
        top = S[rows, 0:128] + GV[:, 0:128]
        for k in range(1, COLS // 128):
            cols = slice(k * 128, (k + 1) * 128)
            top = jnp.maximum(top, S[rows, cols] + GV[:, cols])
        top = jnp.broadcast_to(jnp.max(top, axis=1, keepdims=True), (BLOCK, 128))
        TOPB[rows, :] = top
        total = jnp.zeros((BLOCK, 128), F32)
        for k in range(COLS // 128):
            cols = slice(k * 128, (k + 1) * 128)
            e = jnp.exp2((S[rows, cols] + GV[:, cols]) - top)
            S[rows, cols] = e
            total = total + e
        total = jnp.sum(total, axis=1, keepdims=True)
        RV[0, pl.ds(i, 1), 0] = to_row(top + jnp.log2(total))
        return 0

    lax.fori_loop(0, ROWS // BLOCK, row_one, 0)

    def rr_copy(n, d):
        return copy(
            RV.at[n], RR.at[n, y], rr_send.at[n, d], rr_recv.at[n, y], {"tgt": (y + d) % YS}
        )

    def rr_wait(n, d):
        p = (y + d) % YS
        copy(RV.at[n], RR.at[n, p], rr_send.at[n, d], rr_recv.at[n, p], {"tgt": p}).wait_recv()

    def row_exchange(n):
        for d in range(1, YS):
            rr_copy(n, d).start()
        RR[n, pl.ds(y, 1)] = RV[n][None]
        for d in range(1, YS):
            rr_wait(n, d)
        return RR[n]

    got = row_exchange(0)
    m = jnp.max(got, axis=0)
    lse = m + jnp.log2(jnp.sum(jnp.exp2(got - m[None]), axis=0))
    FV[...] = math.log2(NT) - lse
    for k in range(ROWS // 128):
        rows = pl.ds(k * 128, 128)
        RB[rows, :] = jnp.exp2(TOPB[rows, :] + to_col(FV[k]))

    def col_two(i, total):
        rows = pl.ds(pl.multiple_of(i * STEP, STEP), STEP)
        r = RB[rows, :]
        e = S[rows, :] * jnp.concatenate([r] * (COLS // 128), axis=1)
        S[rows, :] = e
        return total + e[0:8] + e[8:16]

    total = lax.fori_loop(0, ROWS // STEP, col_two, jnp.zeros((8, COLS), F32))
    total = jnp.sum(total, axis=0, keepdims=True)
    for k in range(COLS // 128):
        CV[1, k] = total[:, k * 128 : (k + 1) * 128]
    column_exchange(1, False)
    for k in range(COLS // 128):
        u = CF[1, k]
        g_ref[k] = (EPS * LN2) * (GV[:, k * 128 : (k + 1) * 128] + (math.log2(NS) - jnp.log2(u)))
        GV[:, k * 128 : (k + 1) * 128] = NS / u

    def row_two(i, _):
        rows = pl.ds(pl.multiple_of(i * BLOCK, BLOCK), BLOCK)
        total = jnp.zeros((BLOCK, 128), F32)
        for k in range(COLS // 128):
            cols = slice(k * 128, (k + 1) * 128)
            e = S[rows, cols] * GV[:, cols]
            S[rows, cols] = e
            total = total + e
        RV[1, pl.ds(i, 1), 0] = to_row(jnp.sum(total, axis=1, keepdims=True))
        return 0

    lax.fori_loop(0, ROWS // BLOCK, row_two, 0)
    got = row_exchange(1)
    rho = (got[0] + got[1]) + (got[2] + got[3])
    f_ref[...] = (EPS * LN2) * (FV[...] + (math.log2(NT) - jnp.log2(rho)))
    FV[...] = NT / rho
    for k in range(ROWS // 128):
        rows = pl.ds(k * 128, 128)
        RB[rows, :] = jnp.broadcast_to(to_col(FV[k]), (128, 128))

    MC = 256

    def rm_copy(k, d):
        p = (y + d) % YS
        return copy(
            MT.at[k, p], RM.at[d - 1, k],
            rm_send.at[k, d], rm_recv.at[k, d], {"tgt": p},
        )

    for k in range(ROWS // MC):

        def weigh(i, _, k=k):
            rows = pl.ds(pl.multiple_of(k * MC + i * STEP, STEP), STEP)
            r = RB[rows, :]
            e = S[rows, :] * jnp.concatenate([r] * (COLS // 128), axis=1)
            W[pl.ds(pl.multiple_of(i * STEP, STEP), STEP), :] = e.astype(BF16)
            return 0

        lax.fori_loop(0, MC // STEP, weigh, 0)
        part = dot(GT[...], W[...], NTD) * (1.0 / NT)
        MT[k] = part.reshape(YS, SLAB, MC)
        for d in (2, 1, 3):
            rm_copy(k, d).start()

    grad = jnp.zeros((D, WIDE), F32)
    for k in range(ROWS // MC):
        rest = MT[k].reshape(WIDE, MC)
        for part in range(3):
            piece = rest.astype(BF16)
            grad = grad + dot(ST[:, k * MC : (k + 1) * MC], piece, NTD)
            rest = rest - piece.astype(F32)
    GP[...] = jnp.zeros_like(GP)
    GP[0:D, 0:WIDE] = grad * (EPS * math.sqrt(D) / NS)
    GB[:, 3 * RT8 :] = jnp.zeros((2, TILES - 3 * RT8, 8, 128), F32)
    for h in range(2):
        for t in range(3):
            GB[h, t * RT8 : (t + 1) * RT8] = GP[
                h * RT8 * 8 : (h + 1) * RT8 * 8, t * 128 : (t + 1) * 128
            ].reshape(RT8, 8, 128)

    gc = copy(GB.at[1 - c], GC, gc_send, gc_recv, mate)
    gc.start()
    gc.wait_recv()
    GS[...] = (GB[c] + GC[...]).reshape(CHIPS, 2, 8, 128)

    def gr_copy(d):
        p = ((x + d // ZS) % XS) * ZS + (z + d % ZS) % ZS
        return copy(GS.at[p], GR.at[idx], gr_send.at[d], gr_recv.at[idx], chip(p))

    def gr_wait(d):
        p = ((x + d // ZS) % XS) * ZS + (z + d % ZS) % ZS
        copy(GS.at[p], GR.at[p], gr_send.at[d], gr_recv.at[p], chip(p)).wait_recv()

    for d in FAR:
        gr_copy(d).start()

    GR[pl.ds(idx, 1)] = GS[pl.ds(idx, 1)]

    for d in FAR[::-1]:
        gr_wait(d)

    GO[...] = jnp.sum(GR[...], axis=0)

    def gy_copy(d):
        return copy(GO, GY.at[y], gy_send.at[d], gy_recv.at[y], {"tgt": (y + d) % YS})

    def gy_wait(d):
        p = (y + d) % YS
        copy(GO, GY.at[p], gy_send.at[d], gy_recv.at[p], {"tgt": p}).wait_recv()

    for d in range(1, YS):
        gy_copy(d).start()
    GY[pl.ds(y, 1)] = GO[...][None]
    for d in range(1, YS):
        gy_wait(d)
    GZ[...] = (GY[0] + GY[1]) + (GY[2] + GY[3])

    def gz_copy(d):
        p = ((x + d // ZS) % XS) * ZS + (z + d % ZS) % ZS
        return copy(GZ, GF.at[c, idx], gz_send.at[d], gz_recv.at[idx], chip(p))

    def gz_wait(d):
        p = ((x + d // ZS) % XS) * ZS + (z + d % ZS) % ZS
        copy(GZ, GF.at[c, p], gz_send.at[d], gz_recv.at[p], chip(p)).wait_recv()

    for d in FAR:
        gz_copy(d).start()

    GF[c, pl.ds(idx, 1)] = GZ[...][None]

    for k in range(ROWS // MC):
        for d in range(1, YS):
            rm_copy(k, d).wait_recv()
    for k in range(ROWS // MC):
        m_ref[:, k * MC : (k + 1) * MC] = (
            (MT[k, y] + RM[0, k]) + (RM[1, k] + RM[2, k])
        )[0:75]

    for d in FAR[::-1]:
        gz_wait(d)

    gf = copy(GF.at[c], GF.at[c], gf_send, gf_recv, mate)
    gf.start()
    gf.wait_recv()
    for h in range(2):
        flat = GF[h].reshape(TILES, 8, 128)
        for t in range(3):
            GP[h * RT8 * 8 : (h + 1) * RT8 * 8, t * 128 : (t + 1) * 128] = flat[
                t * RT8 : (t + 1) * RT8
            ].reshape(RT8 * 8, 128)
    for q in range(YS):
        grad_ref[:, q * 75 : (q + 1) * 75] = GP[0:D, q * SLAB : q * SLAB + 75]

    for d in z_order:
        z_copy(d).wait_send()
    for d in x_order:
        for k in range(ZS):
            x_copy(x * ZS + (z + k) % ZS, d, k).wait_send()
        core_copy((x + d) % XS, d).wait_send()
    for d in range(ZS):
        block_copy(x * ZS + (z + d) % ZS, d).wait_send()
    for n in range(2):
        cp_copy(n).wait_send()
        cf_copy(n).wait_send()
        for d in range(1, YS):
            rr_copy(n, d).wait_send()
    for d in range(1, YS):
        gy_copy(d).wait_send()
        for k in range(ROWS // MC):
            rm_copy(k, d).wait_send()
    gc.wait_send()
    gf.wait_send()

    for d in FAR:
        cx_copy(0, d).wait_send()
        cx_copy(1, d).wait_send()
        gr_copy(d).wait_send()
        gz_copy(d).wait_send()


def emit(*refs):
    sems = refs[8]
    copies = [pltpu.make_async_copy(refs[i], refs[4 + i], sems.at[i]) for i in range(4)]
    for one in copies:
        one.start()
    for one in copies:
        one.wait()


def shards(source, target, rotation):
    vmem = pl.BlockSpec(memory_space=pltpu.VMEM)
    dma = pltpu.SemaphoreType.DMA
    scratch = [
        pltpu.VMEM((CHIPS, 2, 32, D), BF16),
        pltpu.VMEM((D, ROWS), BF16),
        pltpu.VMEM((ROWS, D), BF16),
        pltpu.VMEM((D, D), BF16),
        pltpu.VMEM((D, CHUNK), BF16),
        pltpu.VMEM((WIDE, COLS), BF16),
        pltpu.VMEM((ROWS, COLS), F32),
        pltpu.VMEM((256, COLS), BF16),
        pltpu.VMEM((4, YS, SLAB, 256), F32),
        pltpu.VMEM((YS - 1, 4, SLAB, 256), F32),
        pltpu.VMEM((ROWS, 128), F32),
        pltpu.VMEM((ROWS, 128), F32),
        pltpu.VMEM((2, 16, 1, 128), F32),
        pltpu.VMEM((2, 8, 1, 128), F32),
        pltpu.VMEM((2, 8, 1, 128), F32),
        pltpu.VMEM((2, CHIPS, 8, 1, 128), F32),
        pltpu.VMEM((2, 16, 1, 128), F32),
        pltpu.VMEM((1, COLS), F32),
        pltpu.VMEM((2, 8, 1, 128), F32),
        pltpu.VMEM((2, YS, 8, 1, 128), F32),
        pltpu.VMEM((8, 1, 128), F32),
        pltpu.VMEM((2 * RT8 * 8, 384), F32),
        pltpu.VMEM((2, TILES, 8, 128), F32),
        pltpu.VMEM((TILES, 8, 128), F32),
        pltpu.VMEM((CHIPS, 2, 8, 128), F32),
        pltpu.VMEM((CHIPS, 2, 8, 128), F32),
        pltpu.VMEM((2, 8, 128), F32),
        pltpu.VMEM((YS, 2, 8, 128), F32),
        pltpu.VMEM((2, 8, 128), F32),
        pltpu.VMEM((2, CHIPS, 2, 8, 128), F32),
        dma((3,)), dma((ZS,)), dma((CHIPS, 2)), dma((XS, ZS)), dma((XS,)), dma((ZS,)),
        dma((2,)), dma((2,)), dma((2, CHIPS)), dma((2, CHIPS)), dma((2,)), dma((2,)),
        dma((2, YS)), dma((2, YS)), dma((4, YS)), dma((4, YS)),
        dma, dma, dma((CHIPS,)), dma((CHIPS,)), dma((YS,)), dma((YS,)),
        dma((CHIPS,)), dma((CHIPS,)), dma, dma,
    ]
    f, g, m, grad = pl.pallas_call(
        kernel,
        out_shape=(
            jax.ShapeDtypeStruct((8, 1, 128), F32),
            jax.ShapeDtypeStruct((16, 1, 128), F32),
            jax.ShapeDtypeStruct((75, ROWS), F32),
            jax.ShapeDtypeStruct((D, D), F32),
        ),
        in_specs=[pl.BlockSpec(memory_space=pltpu.HBM)] * 3,
        out_specs=(vmem,) * 4,
        scratch_shapes=scratch,
        compiler_params=pltpu.CompilerParams(
            collective_id=0, has_side_effects=True, vmem_limit_bytes=63 << 20
        ),
        name="sinkhorn_step",
    )(source.T, target, rotation)
    f, g, m, grad = pl.pallas_call(
        emit,
        out_shape=tuple(jax.ShapeDtypeStruct(a.shape, a.dtype) for a in (f, g, m, grad)),
        in_specs=[vmem] * 4,
        out_specs=(pl.BlockSpec(memory_space=pl.ANY),) * 4,
        scratch_shapes=[dma((4,))],
        name="write_results",
    )(f, g, m, grad)
    return (f.reshape(ROWS), g.reshape(COLS), m.T, grad)


def solution(mesh):
    placed = (P("src", None), P(("tgt", "src"), None), P())
    return jax.shard_map(
        shards,
        mesh=mesh,
        in_specs=placed,
        out_specs=(P("src"), P("tgt"), P("src", "tgt"), P()),
        check_vma=False,
    )
```
